512 devices in a mesh: dp: 64 (over z, x, core), tensor: 8 (over y).
Axes of the slice: x: 4, y: 8, z: 8, core: 2. Of those that a mesh axis runs over, the one named last changes fastest.
Arguments:
- grads: bfloat16 [64, 256, 8192], P('dp', 'tensor')
- error: float32 [64, 256, 8192], P('dp', 'tensor'), may hold values from -3 to 3
- q_init: float32 [256, 16], P('tensor'), may hold values from -6 to 6
Outputs:
- update: bfloat16 [256, 8192], P('tensor')
- new_error: float32 [64, 256, 8192], P('dp', 'tensor')
- new_q: float32 [256, 16], P('tensor')
The draws below stay inside these ranges and needn't reach their ends.
All inputs are finite; a program needn't handle non-finite values.
Results may differ from the reference program's by a relative error of at most 0.001.
Values sent between devices are 32-bit elements; how exact they have to be, the bound alone decides.
No kernel may reach another device: no remote copies, remote signals or barrier semaphores. Data moves between devices by JAX's collectives and lax.ppermute only.
A program may use at most 64 MiB of HBM per device.

```python
import jax
import jax.numpy as jnp
from jax import lax

D = 8192
R = 16
COLS = 256
REPLICAS = 64


def draw_grads(key, part):
    key = jax.random.fold_in(key, 7)
    spread = jnp.exp(jax.random.uniform(jax.random.fold_in(key, 3), (1, 1, D), jnp.float32, 0.0, 2.3))
    common = jax.random.normal(jax.random.fold_in(key, 1), (1, COLS, D), jnp.float32)
    own = jax.random.normal(jax.random.fold_in(key, 2), (REPLICAS, COLS, D), jnp.float32)
    mixed = common + 0.6 * own
    return (mixed * spread * 0.3).astype(jnp.bfloat16)


def levels(key, extent, cuts, low, high):
    gain = 1.0
    for position, blocks in cuts:
        draws = jax.random.uniform(jax.random.fold_in(jax.random.fold_in(key, 6), position), (blocks,), jnp.float32, low / len(cuts), high / len(cuts))
        gain = gain * jnp.repeat(jnp.exp(draws), extent[position] // blocks).reshape((-1,) + (1,) * (len(extent) - 1 - position))
    return gain


def scatter_about(own_key, shape, deviation, reach, pieces=(), kind=jnp.bfloat16):
    drawn = deviation * jax.random.normal(own_key, shape, jnp.float32)
    if pieces:
        drawn = drawn * levels(own_key, shape, pieces, -0.22, 0.18)
    return jnp.clip(drawn, -reach, reach).astype(kind)


def setup_inputs(seed: int = 0) -> dict:
    keys = jax.random.split(jax.random.key(seed), 4)
    grads = draw_grads(jax.random.fold_in(keys[3], 71), 0)
    error = scatter_about(keys[1], (REPLICAS, COLS, D), 0.3, 3.0, ((0, 64), (1, 8)), jnp.float32)
    q_init = scatter_about(keys[2], (COLS, R), 1.0, 6.0, ((0, 8),), jnp.float32)
    return dict(grads=grads, error=error, q_init=q_init)


def reference(grads, error, q_init):

    def add_left(total, pair):
        merged = pair[0].astype(jnp.float32) + pair[1]
        return (total + jnp.dot(merged.T, q_init, precision=lax.Precision.HIGHEST), None)
    left, unused = lax.scan(add_left, jnp.zeros((D, R), jnp.float32), (grads, error))
    gram = jnp.dot(left.T, left, precision=lax.Precision.HIGHEST)
    ridge = 1e-06 * jnp.trace(gram) / R
    lower = jnp.linalg.cholesky(gram + ridge * jnp.eye(R, dtype=jnp.float32))
    ortho = lax.linalg.triangular_solve(lower, left, left_side=False, lower=True, transpose_a=True)

    def add_right(total, pair):
        merged = pair[0].astype(jnp.float32) + pair[1]
        return (total + jnp.dot(merged, ortho, precision=lax.Precision.HIGHEST), None)
    right, unused = lax.scan(add_right, jnp.zeros((COLS, R), jnp.float32), (grads, error))
    new_q = right / REPLICAS
    approx = jnp.dot(new_q, ortho.T, precision=lax.Precision.HIGHEST)

    def residual_of(pair):
        return pair[0].astype(jnp.float32) + pair[1] - approx
    new_error = lax.map(residual_of, (grads, error))
    return (approx.astype(jnp.bfloat16), new_error, new_q)
```

```python
import jax
import jax.numpy as jnp
from jax import lax
from jax.sharding import PartitionSpec as P

HIGHEST = lax.Precision.HIGHEST
LANES = 128


def swap_cores(value):
    count = lax.axis_size("dp")
    return lax.ppermute(value, "dp", [(i, i ^ 1) for i in range(count)])


def across_chips(value):
    count = lax.axis_size("dp")
    groups = [list(range(core, count, 2)) for core in range(2)]
    return lax.all_to_all(value, "dp", 0, 0, axis_index_groups=groups)


def per_device(grads, error, q_init):
    replicas = lax.axis_size("dp")
    shards = lax.axis_size("tensor")
    chips = replicas // 2
    cols, depth = grads.shape[1:]
    rank = q_init.shape[1]
    core = lax.axis_index("dp") % 2
    merged = grads[0].astype(jnp.float32) + error[0]
    halves = merged.reshape(cols, 2, chips, LANES).transpose(1, 2, 0, 3)
    mine = lax.dynamic_index_in_dim(halves, core, 0, keepdims=False)
    other = lax.dynamic_index_in_dim(halves, 1 - core, 0, keepdims=False)
    pair = mine + swap_cores(other)
    total = across_chips(pair).sum(0)
    part = jnp.dot(q_init.T, total, precision=HIGHEST)
    parts = lax.all_to_all(jnp.broadcast_to(part, (shards, rank, LANES)), "tensor", 0, 0)
    left = parts.sum(0)
    peak = jnp.maximum(jnp.max(jnp.abs(left)), 1e-30)
    small = jnp.dot(left / peak, total.T, precision=HIGHEST)
    gram = jnp.dot(left, left.T, precision=HIGHEST)
    packed = jnp.concatenate([small, gram, jnp.full((rank, 64 - cols - rank), peak)], axis=1)
    packed = jnp.concatenate([packed[: rank // 2], packed[rank // 2 :]], axis=1)
    message = jnp.concatenate([left, packed], axis=0)
    own = across_chips(jnp.broadcast_to(message, (chips,) + message.shape))
    got = swap_cores(own)
    first = jnp.where(core == 0, own, got)
    second = jnp.where(core == 0, got, own)
    every = jnp.concatenate([first, second], axis=0)
    left_all = every[:, :rank].transpose(1, 0, 2).reshape(rank, depth)
    packed = every[:, rank:]
    packed = jnp.concatenate([packed[:, :, :64], packed[:, :, 64:]], axis=1)
    peaks = packed[:, :1, 48:49]
    peak = jnp.max(peaks)
    small = (packed[:, :, :cols] * (peaks / peak)).sum(0)
    gram = packed[:, :, cols : cols + rank].sum(0)
    ridge = 1e-06 * jnp.trace(gram) / rank
    lower = jnp.linalg.cholesky(gram + ridge * jnp.eye(rank, dtype=jnp.float32)) / peak
    new_q = lax.linalg.triangular_solve(lower, small, left_side=True, lower=True) / replicas
    coef = lax.linalg.triangular_solve(lower, new_q, left_side=True, lower=True, transpose_a=True) / peak
    approx = jnp.dot(coef.T, left_all, precision=HIGHEST)
    return (approx.astype(jnp.bfloat16), (merged - approx)[None], new_q.T)


def solution(mesh):
    in_specs = (P("dp", "tensor", None), P("dp", "tensor", None), P("tensor", None))
    out_specs = (P("tensor", None), P("dp", "tensor", None), P("tensor", None))
    return jax.shard_map(
        per_device, mesh=mesh, in_specs=in_specs, out_specs=out_specs, check_vma=False
    )
```

```python
import functools

import jax
import jax.numpy as jnp
from jax import lax
from jax.experimental import pallas as pl
from jax.experimental.pallas import tpu as pltpu
from jax.sharding import PartitionSpec as P

HIGHEST = lax.Precision.HIGHEST
LANES = 128
HALF = LANES // 2
VMEM = pl.BlockSpec(memory_space=pltpu.VMEM)
SMEM = pl.BlockSpec(memory_space=pltpu.SMEM)
ANY = pl.BlockSpec(memory_space=pl.ANY)
VMEM_LIMIT = 12 * 2**20


def swap_cores(value):
    count = lax.axis_size("dp")
    return lax.ppermute(value, "dp", [(i, i ^ 1) for i in range(count)])


def across_chips(value):
    count = lax.axis_size("dp")
    groups = [list(range(core, count, 2)) for core in range(2)]
    return lax.all_to_all(value, "dp", 0, 0, axis_index_groups=groups)


def merge_kernel(half_ref, grads, error, out, grad_buf, error_buf, sems):
    chips = out.shape[0]
    pieces = grad_buf.shape[0]
    width = grad_buf.shape[2]
    start = half_ref[0] * (chips * LANES)
    copies = []
    for i in range(pieces):
        at = pl.ds(pl.multiple_of(start + i * width, LANES), width)
        one = pltpu.make_async_copy(grads.at[:, at], grad_buf.at[i], sems.at[0, i])
        two = pltpu.make_async_copy(error.at[:, at], error_buf.at[i], sems.at[1, i])
        one.start()
        two.start()
        copies.append((one, two))
    for i in range(pieces):
        for copy in copies[i]:
            copy.wait()
        for j in range(width // LANES):
            at = slice(j * LANES, (j + 1) * LANES)
            out[i * (width // LANES) + j] = grad_buf[i, :, at].astype(jnp.float32) + error_buf[i, :, at]


def merged_half(half, grads, error):
    cols, depth = grads.shape
    chips = depth // (2 * LANES)
    pieces = 2
    width = depth // 2 // pieces
    return pl.pallas_call(
        merge_kernel,
        out_shape=jax.ShapeDtypeStruct((chips, cols, LANES), jnp.float32),
        in_specs=[SMEM, ANY, ANY],
        out_specs=VMEM,
        scratch_shapes=[
            pltpu.VMEM((pieces, cols, width), grads.dtype),
            pltpu.VMEM((pieces, cols, width), jnp.float32),
            pltpu.SemaphoreType.DMA((2, pieces)),
        ],
        compiler_params=pltpu.CompilerParams(vmem_limit_bytes=VMEM_LIMIT),
        cost_estimate=pl.CostEstimate(flops=cols * depth, bytes_accessed=5 * cols * depth, transcendentals=0),
        name="merge",
    )(half.reshape(1), grads, error)


def message_kernel(parts, total, out):
    rank = parts.shape[1]
    cols = total.shape[0]
    left = parts[0]
    for i in range(1, parts.shape[0]):
        left = left + parts[i]
    peak = jnp.max(jnp.max(jnp.abs(left), axis=0, keepdims=True), axis=1, keepdims=True)
    peak = jnp.maximum(peak, 1e-30)
    scaled = left / peak
    pad = jnp.zeros((LANES - cols - rank, LANES), jnp.float32)
    other = jnp.concatenate([total[...], scaled, pad], axis=0)
    prods = lax.dot_general(scaled, other, (((1,), (1,)), ((), ())), precision=HIGHEST, preferred_element_type=jnp.float32)
    lane = lax.broadcasted_iota(jnp.int32, prods.shape, 1)
    prods = jnp.where(lane < cols, prods, jnp.where(lane < cols + rank, prods * peak * peak, jnp.broadcast_to(peak, prods.shape)))
    low = prods[: rank // 2]
    high = pltpu.roll(prods[rank // 2 :], HALF, 1)
    packed = jnp.where(lane[: rank // 2] < HALF, low, high)
    for i in range(out.shape[0]):
        out[i, :rank, :] = left
        out[i, rank:, :] = packed


def message_of(parts, total, chips):
    rank = parts.shape[1]
    return pl.pallas_call(
        message_kernel,
        out_shape=jax.ShapeDtypeStruct((chips, rank + rank // 2, LANES), jnp.float32),
        in_specs=[VMEM, VMEM],
        out_specs=VMEM,
        compiler_params=pltpu.CompilerParams(vmem_limit_bytes=VMEM_LIMIT),
        name="message",
    )(parts, total)


def split3(value):
    first = value.astype(jnp.bfloat16)
    rest = value - first.astype(jnp.float32)
    second = rest.astype(jnp.bfloat16)
    third = (rest - second.astype(jnp.float32)).astype(jnp.bfloat16)
    return first, second, third


def solve(own, got, rank, cols, replicas):
    blocks = jnp.concatenate([own[:, rank:, :], got[:, rank:, :]], axis=0)
    peaks = blocks[:, :, cols + rank : cols + rank + 1]
    own_peaks, got_peaks = peaks[: own.shape[0]], peaks[own.shape[0] :]
    peak = jnp.max(peaks, axis=0)
    weights = peaks / peak[None]
    weighted = blocks * weights
    count = own.shape[0]
    small = jnp.sum(weighted[:count], axis=0) + jnp.sum(weighted[count:], axis=0)
    gram = jnp.sum(blocks[:count], axis=0) + jnp.sum(blocks[count:], axis=0)
    small = jnp.concatenate([small, pltpu.roll(small, HALF, 1)], axis=0)
    gram = jnp.concatenate([gram, pltpu.roll(gram, HALF, 1)], axis=0)
    shape = (rank, LANES)
    peak = jnp.broadcast_to(peak[:1], (1, LANES))
    row = lax.broadcasted_iota(jnp.int32, shape, 0)
    column = [jnp.broadcast_to(gram[:, cols + j : cols + j + 1], shape) for j in range(rank)]
    trace = column[0][:1]
    for j in range(1, rank):
        trace = trace + column[j][j : j + 1]
    ridge = 1e-06 * trace / rank
    column = [jnp.where(row == j, column[j] + ridge, column[j]) for j in range(rank)]
    root = jnp.zeros(shape, jnp.float32)
    for k in range(rank):
        pivot = column[k][k : k + 1]
        inverse = 1.0 / pivot
        root = jnp.where(row == k, jnp.sqrt(inverse), root)
        factor = jnp.where(row > k, column[k] * inverse, 0.0)
        for j in range(k + 1, rank):
            column[j] = column[j] - factor * column[j][k : k + 1]
        small = small - factor * small[k : k + 1]
    new_q = small * (peak * root * (1.0 / replicas))
    coef = new_q * root
    for k in range(rank - 1, 0, -1):
        upper = jnp.where(row < k, column[k] * root * root, 0.0)
        coef = coef - upper * coef[k : k + 1]
    return new_q, coef


def finish_kernel(replicas, core_ref, own, got, grads, error, update, residual, new_q_ref,
                  grad_buf, error_buf, update_buf, residual_buf, in_sems, out_sems):
    chips, cols, rank = own.shape[0], grads.shape[0], new_q_ref.shape[0]
    span = chips * LANES
    pieces = out_sems.shape[2]
    width = span // pieces
    starts = [pl.multiple_of(core_ref[0] * span, LANES), pl.multiple_of((1 - core_ref[0]) * span, LANES)]
    loads = []
    for h in range(2):
        one = pltpu.make_async_copy(grads.at[:, pl.ds(starts[h], span)], grad_buf.at[h], in_sems.at[0, h])
        two = pltpu.make_async_copy(error.at[:, pl.ds(starts[h], span)], error_buf.at[h], in_sems.at[1, h])
        one.start()
        two.start()
        loads.append((one, two))
    new_q, coef = solve(own, got, rank, cols, replicas)
    new_q_ref[...] = new_q[:, :cols]
    first, second, third = split3(coef)
    lhs = jnp.concatenate([first, first, second, first, second, third], axis=0)
    lhs = jnp.transpose(lhs.astype(jnp.float32))[:cols].astype(jnp.bfloat16)
    stores = []
    for h in range(2):
        source = own if h == 0 else got
        for copy in loads[h]:
            copy.wait()
        for i in range(chips // 2):
            at = slice(i * 2 * LANES, (i + 1) * 2 * LANES)
            left = jnp.concatenate([source[2 * i, :rank, :], source[2 * i + 1, :rank, :]], axis=1)
            one, two, three = split3(left)
            rhs = jnp.concatenate([one, two, one, three, two, one], axis=0)
            approx = jnp.dot(lhs, rhs, preferred_element_type=jnp.float32)
            update_buf[h, :, at] = approx.astype(jnp.bfloat16)
            residual_buf[h, :, at] = (grad_buf[h, :, at].astype(jnp.float32) + error_buf[h, :, at]) - approx
            done = (i + 1) * 2 * LANES
            if done % width == 0:
                piece = done // width - 1
                here = pl.ds(piece * width, width)
                there = pl.ds(pl.multiple_of(starts[h] + piece * width, LANES), width)
                three = pltpu.make_async_copy(update_buf.at[h, :, here], update.at[:, there], out_sems.at[0, h, piece])
                four = pltpu.make_async_copy(residual_buf.at[h, :, here], residual.at[:, there], out_sems.at[1, h, piece])
                three.start()
                four.start()
                stores += [three, four]
    for copy in stores:
        copy.wait()


def finish(core, own, got, grads, error, rank, replicas):
    cols, depth = grads.shape
    span = depth // 2
    pieces = 2
    return pl.pallas_call(
        functools.partial(finish_kernel, replicas),
        out_shape=(
            jax.ShapeDtypeStruct((cols, depth), jnp.bfloat16),
            jax.ShapeDtypeStruct((cols, depth), jnp.float32),
            jax.ShapeDtypeStruct((rank, cols), jnp.float32),
        ),
        in_specs=[SMEM, VMEM, VMEM, ANY, ANY],
        out_specs=(ANY, ANY, VMEM),
        scratch_shapes=[
            pltpu.VMEM((2, cols, span), jnp.bfloat16),
            pltpu.VMEM((2, cols, span), jnp.float32),
            pltpu.VMEM((2, cols, span), jnp.bfloat16),
            pltpu.VMEM((2, cols, span), jnp.float32),
            pltpu.SemaphoreType.DMA((2, 2)),
            pltpu.SemaphoreType.DMA((2, 2, pieces)),
        ],
        compiler_params=pltpu.CompilerParams(vmem_limit_bytes=VMEM_LIMIT),
        name="finish",
    )(core.reshape(1), own, got, grads, error)


def per_device(grads, error, q_init):
    replicas = lax.axis_size("dp")
    shards = lax.axis_size("tensor")
    chips = replicas // 2
    rank = q_init.shape[1]
    grads, error = grads[0], error[0]
    core = lax.axis_index("dp") % 2
    other = merged_half(1 - core, grads, error)
    swapped = swap_cores(other)
    mine = merged_half(core, grads, error)
    total = across_chips(mine + swapped).sum(0)
    part = jnp.dot(q_init.T, total, precision=HIGHEST)
    parts = lax.all_to_all(jnp.broadcast_to(part, (shards, rank, LANES)), "tensor", 0, 0)
    own = across_chips(message_of(parts, total, chips))
    got = swap_cores(own)
    update, residual, new_q = finish(core, own, got, grads, error, rank, replicas)
    return update, residual[None], new_q.T


def solution(mesh):
    in_specs = (P("dp", "tensor", None), P("dp", "tensor", None), P("tensor", None))
    out_specs = (P("tensor", None), P("dp", "tensor", None), P("tensor", None))
    return jax.shard_map(
        per_device, mesh=mesh, in_specs=in_specs, out_specs=out_specs, check_vma=False
    )
```

```python
import functools

import jax
import jax.numpy as jnp
from jax import lax
from jax.experimental import pallas as pl
from jax.experimental.pallas import tpu as pltpu
from jax.sharding import PartitionSpec as P

HIGHEST = lax.Precision.HIGHEST
LANES = 128
HALF = LANES // 2
VMEM = pl.BlockSpec(memory_space=pltpu.VMEM)
SMEM = pl.BlockSpec(memory_space=pltpu.SMEM)
ANY = pl.BlockSpec(memory_space=pl.ANY)
HBM = pl.BlockSpec(memory_space=pltpu.HBM)
VMEM_LIMIT = 12 * 2**20


def swap_cores(value):
    count = lax.axis_size("dp")
    return lax.ppermute(value, "dp", [(i, i ^ 1) for i in range(count)])


def across_chips(value):
    count = lax.axis_size("dp")
    groups = [list(range(core, count, 2)) for core in range(2)]
    return lax.all_to_all(value, "dp", 0, 0, axis_index_groups=groups)


def merge_kernel(half_ref, grads, error, out, grad_buf, error_buf, sems):
    chips = out.shape[0]
    pieces = grad_buf.shape[0]
    width = grad_buf.shape[2]
    start = half_ref[0] * (chips * LANES)
    copies = []
    for i in range(pieces):
        at = pl.ds(pl.multiple_of(start + i * width, LANES), width)
        one = pltpu.make_async_copy(grads.at[:, at], grad_buf.at[i], sems.at[0, i])
        two = pltpu.make_async_copy(error.at[:, at], error_buf.at[i], sems.at[1, i])
        one.start()
        two.start()
        copies.append((one, two))
    for i in range(pieces):
        for copy in copies[i]:
            copy.wait()
        for j in range(width // LANES):
            at = slice(j * LANES, (j + 1) * LANES)
            out[i * (width // LANES) + j] = grad_buf[i, :, at].astype(jnp.float32) + error_buf[i, :, at]


def merged_half(half, grads, error):
    cols, depth = grads.shape
    chips = depth // (2 * LANES)
    pieces = 2
    width = depth // 2 // pieces
    return pl.pallas_call(
        merge_kernel,
        out_shape=jax.ShapeDtypeStruct((chips, cols, LANES), jnp.float32),
        in_specs=[SMEM, HBM, HBM],
        out_specs=VMEM,
        scratch_shapes=[
            pltpu.VMEM((pieces, cols, width), grads.dtype),
            pltpu.VMEM((pieces, cols, width), jnp.float32),
            pltpu.SemaphoreType.DMA((2, pieces)),
        ],
        compiler_params=pltpu.CompilerParams(vmem_limit_bytes=VMEM_LIMIT),
        cost_estimate=pl.CostEstimate(flops=cols * depth, bytes_accessed=5 * cols * depth, transcendentals=0),
        name="merge",
    )(half.reshape(1), *(pltpu.with_memory_space_constraint(x, pltpu.HBM) for x in (grads, error)))


def message_kernel(parts, total, out):
    rank = parts.shape[1]
    cols = total.shape[0]
    left = parts[0]
    for i in range(1, parts.shape[0]):
        left = left + parts[i]
    peak = jnp.max(jnp.max(jnp.abs(left), axis=0, keepdims=True), axis=1, keepdims=True)
    peak = jnp.maximum(peak, 1e-30)
    scaled = left / peak
    pad = jnp.zeros((LANES - cols - rank, LANES), jnp.float32)
    other = jnp.concatenate([total[...], scaled, pad], axis=0)
    prods = lax.dot_general(scaled, other, (((1,), (1,)), ((), ())), precision=HIGHEST, preferred_element_type=jnp.float32)
    lane = lax.broadcasted_iota(jnp.int32, prods.shape, 1)
    prods = jnp.where(lane < cols, prods, jnp.where(lane < cols + rank, prods * peak * peak, jnp.broadcast_to(peak, prods.shape)))
    low = prods[: rank // 2]
    high = pltpu.roll(prods[rank // 2 :], HALF, 1)
    packed = jnp.where(lane[: rank // 2] < HALF, low, high)
    for i in range(out.shape[0]):
        out[i, :rank, :] = left
        out[i, rank:, :] = packed


def message_of(parts, total, chips):
    rank = parts.shape[1]
    return pl.pallas_call(
        message_kernel,
        out_shape=jax.ShapeDtypeStruct((chips, rank + rank // 2, LANES), jnp.float32),
        in_specs=[VMEM, VMEM],
        out_specs=VMEM,
        compiler_params=pltpu.CompilerParams(vmem_limit_bytes=VMEM_LIMIT),
        name="message",
    )(parts, total)


def split3(value):
    first = value.astype(jnp.bfloat16)
    rest = value - first.astype(jnp.float32)
    second = rest.astype(jnp.bfloat16)
    third = (rest - second.astype(jnp.float32)).astype(jnp.bfloat16)
    return first, second, third


def solve(own, got, rank, cols, replicas):
    blocks = jnp.concatenate([own[:, rank:, :], got[:, rank:, :]], axis=0)
    peaks = blocks[:, :, cols + rank : cols + rank + 1]
    own_peaks, got_peaks = peaks[: own.shape[0]], peaks[own.shape[0] :]
    peak = jnp.max(peaks, axis=0)
    weights = peaks / peak[None]
    weighted = blocks * weights
    count = own.shape[0]
    small = jnp.sum(weighted[:count], axis=0) + jnp.sum(weighted[count:], axis=0)
    gram = jnp.sum(blocks[:count], axis=0) + jnp.sum(blocks[count:], axis=0)
    small = jnp.concatenate([small, pltpu.roll(small, HALF, 1)], axis=0)
    gram = jnp.concatenate([gram, pltpu.roll(gram, HALF, 1)], axis=0)
    shape = (rank, LANES)
    peak = jnp.broadcast_to(peak[:1], (1, LANES))
    row = lax.broadcasted_iota(jnp.int32, shape, 0)
    column = [jnp.broadcast_to(gram[:, cols + j : cols + j + 1], shape) for j in range(rank)]
    trace = column[0][:1]
    for j in range(1, rank):
        trace = trace + column[j][j : j + 1]
    ridge = 1e-06 * trace / rank
    column = [jnp.where(row == j, column[j] + ridge, column[j]) for j in range(rank)]
    root = jnp.zeros(shape, jnp.float32)
    for k in range(rank):
        pivot = column[k][k : k + 1]
        inverse = 1.0 / pivot
        root = jnp.where(row == k, jnp.sqrt(inverse), root)
        factor = jnp.where(row > k, column[k] * inverse, 0.0)
        for j in range(k + 1, rank):
            column[j] = column[j] - factor * column[j][k : k + 1]
        small = small - factor * small[k : k + 1]
    new_q = small * (peak * root * (1.0 / replicas))
    coef = new_q * root
    for k in range(rank - 1, 0, -1):
        upper = jnp.where(row < k, column[k] * root * root, 0.0)
        coef = coef - upper * coef[k : k + 1]
    return new_q, coef


def finish_kernel(replicas, core_ref, own, got, mine, other, update, residual, new_q_ref,
                  update_buf, residual_buf, sems):
    chips, cols = mine.shape[:2]
    rank = new_q_ref.shape[0]
    span = chips * LANES
    pieces = sems.shape[2]
    width = span // pieces
    starts = [pl.multiple_of(core_ref[0] * span, LANES), pl.multiple_of((1 - core_ref[0]) * span, LANES)]
    new_q, coef = solve(own, got, rank, cols, replicas)
    new_q_ref[...] = new_q[:, :cols]
    first, second, third = split3(coef)
    lhs = jnp.concatenate([first, first, second, first, second, third], axis=0)
    lhs = jnp.transpose(lhs.astype(jnp.float32))[:cols].astype(jnp.bfloat16)
    stores = []
    for h, (source, merged) in enumerate(((own, mine), (got, other))):
        for i in range(0, chips, 2):
            left = jnp.concatenate([source[i, :rank, :], source[i + 1, :rank, :]], axis=1)
            one, two, three = split3(left)
            rhs = jnp.concatenate([one, two, one, three, two, one], axis=0)
            approx = jnp.dot(lhs, rhs, preferred_element_type=jnp.float32)
            at = slice(i * LANES, (i + 2) * LANES)
            update_buf[h, :, at] = approx.astype(jnp.bfloat16)
            residual_buf[h, :, at] = jnp.concatenate([merged[i], merged[i + 1]], axis=1) - approx
            done = (i + 2) * LANES
            if done % width == 0:
                piece = done // width - 1
                here = pl.ds(piece * width, width)
                there = pl.ds(pl.multiple_of(starts[h] + piece * width, LANES), width)
                one = pltpu.make_async_copy(update_buf.at[h, :, here], update.at[:, there], sems.at[0, h, piece])
                two = pltpu.make_async_copy(residual_buf.at[h, :, here], residual.at[:, there], sems.at[1, h, piece])
                one.start()
                two.start()
                stores += [one, two]
    for copy in stores:
        copy.wait()


def finish(core, own, got, mine, other, rank, replicas):
    chips, cols = mine.shape[:2]
    span = chips * LANES
    pieces = 2
    return pl.pallas_call(
        functools.partial(finish_kernel, replicas),
        out_shape=(
            jax.ShapeDtypeStruct((cols, 2 * span), jnp.bfloat16),
            jax.ShapeDtypeStruct((cols, 2 * span), jnp.float32),
            jax.ShapeDtypeStruct((rank, cols), jnp.float32),
        ),
        in_specs=[SMEM, VMEM, VMEM, VMEM, VMEM],
        out_specs=(ANY, ANY, VMEM),
        scratch_shapes=[
            pltpu.VMEM((2, cols, span), jnp.bfloat16),
            pltpu.VMEM((2, cols, span), jnp.float32),
            pltpu.SemaphoreType.DMA((2, 2, pieces)),
        ],
        compiler_params=pltpu.CompilerParams(vmem_limit_bytes=VMEM_LIMIT),
        name="finish",
    )(core.reshape(1), own, got, mine, other)


def per_device(grads, error, q_init):
    replicas = lax.axis_size("dp")
    shards = lax.axis_size("tensor")
    chips = replicas // 2
    rank = q_init.shape[1]
    grads, error = grads[0], error[0]
    core = lax.axis_index("dp") % 2
    other = merged_half(1 - core, grads, error)
    swapped = swap_cores(other)
    mine = merged_half(core, grads, error)
    total = across_chips(mine + swapped).sum(0)
    part = jnp.dot(q_init.T, total, precision=HIGHEST)
    parts = lax.all_to_all(jnp.broadcast_to(part, (shards, rank, LANES)), "tensor", 0, 0)
    own = across_chips(message_of(parts, total, chips))
    got = swap_cores(own)
    update, residual, new_q = finish(core, own, got, mine, other, rank, replicas)
    return update, residual[None], new_q.T


def solution(mesh):
    in_specs = (P("dp", "tensor", None), P("dp", "tensor", None), P("tensor", None))
    out_specs = (P("tensor", None), P("dp", "tensor", None), P("tensor", None))
    return jax.shard_map(
        per_device, mesh=mesh, in_specs=in_specs, out_specs=out_specs, check_vma=False
    )
```

```python
import functools

import jax
import jax.numpy as jnp
from jax import lax
from jax.experimental import pallas as pl
from jax.experimental.pallas import tpu as pltpu
from jax.sharding import PartitionSpec as P

HIGHEST = lax.Precision.HIGHEST
LANES = 128
QUARTER = LANES // 4
TILE = 4
VMEM = pl.BlockSpec(memory_space=pltpu.VMEM)
SMEM = pl.BlockSpec(memory_space=pltpu.SMEM)
ANY = pl.BlockSpec(memory_space=pl.ANY)
HBM = pl.BlockSpec(memory_space=pltpu.HBM)
VMEM_LIMIT = 12 * 2**20


def swap_cores(value):
    count = lax.axis_size("dp")
    return lax.ppermute(value, "dp", [(i, i ^ 1) for i in range(count)])


def across_chips(value):
    count = lax.axis_size("dp")
    groups = [list(range(core, count, 2)) for core in range(2)]
    return lax.all_to_all(value, "dp", 0, 0, axis_index_groups=groups)


def merge_kernel(half_ref, grads, error, out, grad_buf, error_buf, sems):
    chips = out.shape[0]
    pieces = grad_buf.shape[0]
    width = grad_buf.shape[2]
    start = half_ref[0] * (chips * LANES)
    copies = []
    for i in range(pieces):
        at = pl.ds(pl.multiple_of(start + i * width, LANES), width)
        one = pltpu.make_async_copy(grads.at[:, at], grad_buf.at[i], sems.at[0, i])
        two = pltpu.make_async_copy(error.at[:, at], error_buf.at[i], sems.at[1, i])
        one.start()
        two.start()
        copies.append((one, two))
    for i in range(pieces):
        for copy in copies[i]:
            copy.wait()
        for j in range(width // LANES):
            at = slice(j * LANES, (j + 1) * LANES)
            out[i * (width // LANES) + j] = grad_buf[i, :, at].astype(jnp.float32) + error_buf[i, :, at]


def merged_half(half, grads, error):
    cols, depth = grads.shape
    chips = depth // (2 * LANES)
    pieces = 2
    width = depth // 2 // pieces
    return pl.pallas_call(
        merge_kernel,
        out_shape=jax.ShapeDtypeStruct((chips, cols, LANES), jnp.float32),
        in_specs=[SMEM, HBM, HBM],
        out_specs=VMEM,
        scratch_shapes=[
            pltpu.VMEM((pieces, cols, width), grads.dtype),
            pltpu.VMEM((pieces, cols, width), jnp.float32),
            pltpu.SemaphoreType.DMA((2, pieces)),
        ],
        compiler_params=pltpu.CompilerParams(vmem_limit_bytes=VMEM_LIMIT),
        cost_estimate=pl.CostEstimate(flops=cols * depth, bytes_accessed=5 * cols * depth, transcendentals=0),
        name="merge",
    )(half.reshape(1), *(pltpu.with_memory_space_constraint(x, pltpu.HBM) for x in (grads, error)))


def message_kernel(parts, total, out):
    chips, tiles = out.shape[:2]
    left = parts[0]
    for i in range(1, parts.shape[0]):
        left = left + parts[i]
    scaled = left / peak_of(left)
    pad = jnp.zeros((LANES - total.shape[0], LANES), jnp.float32)
    other = jnp.concatenate([total[...], pad], axis=0)
    small = lax.dot_general(scaled, other, (((1,), (1,)), ((), ())), precision=HIGHEST, preferred_element_type=jnp.float32)
    lane = lax.broadcasted_iota(jnp.int32, (TILE, LANES), 1)
    packed = small[:TILE]
    for j in range(1, tiles - 1):
        piece = pltpu.roll(small, j * QUARTER, 1)[j * TILE : (j + 1) * TILE]
        packed = jnp.where(lane >= j * QUARTER, piece, packed)
    pieces = [left[j * TILE : (j + 1) * TILE] for j in range(tiles - 1)] + [packed]
    for i in range(chips):
        for j in range(tiles):
            out[i, j] = pieces[j]


def message_of(parts, total, chips):
    tiles = parts.shape[1] // TILE + 1
    return pl.pallas_call(
        message_kernel,
        out_shape=jax.ShapeDtypeStruct((chips, tiles, TILE, LANES), jnp.float32),
        in_specs=[VMEM, VMEM],
        out_specs=VMEM,
        compiler_params=pltpu.CompilerParams(vmem_limit_bytes=VMEM_LIMIT),
        name="message",
    )(parts, total)


def peak_of(left):
    peak = jnp.max(jnp.max(jnp.abs(left), axis=1, keepdims=True), axis=0, keepdims=True)
    return jnp.maximum(peak, 1e-30)


def split3(value):
    first = value.astype(jnp.bfloat16)
    rest = value - first.astype(jnp.float32)
    second = rest.astype(jnp.bfloat16)
    third = (rest - second.astype(jnp.float32)).astype(jnp.bfloat16)
    return first, second, third


def left_of(message, i):
    tiles = message.shape[1] - 1
    return jnp.concatenate([message[i, j] for j in range(tiles)], axis=0)


def sums_of(message):
    chips, tiles = message.shape[0], message.shape[1] - 1
    rank = tiles * TILE
    square = jnp.zeros((3 * rank, 3 * rank), jnp.float32)
    peaks = []
    for i in range(0, chips, 2):
        pair = [left_of(message, i), left_of(message, i + 1)]
        peaks += [jnp.broadcast_to(peak_of(left), (1, LANES)) for left in pair]
        terms = jnp.concatenate(split3(jnp.concatenate(pair, axis=1)), axis=0)
        square += lax.dot_general(terms, terms, (((1,), (1,)), ((), ())), preferred_element_type=jnp.float32)
    at = [slice(i * rank, (i + 1) * rank) for i in range(3)]
    cross = square[at[0], at[2]] + square[at[2], at[0]] + square[at[1], at[1]]
    cross = cross + (square[at[0], at[1]] + square[at[1], at[0]])
    gram = square[at[0], at[0]] + cross
    gram = jnp.concatenate([gram, jnp.zeros((rank, LANES - rank), jnp.float32)], axis=1)
    peak = functools.reduce(jnp.maximum, peaks)
    inverse = 1.0 / peak
    small = functools.reduce(jnp.add, [message[i, tiles] * (peaks[i] * inverse) for i in range(chips)])
    small = jnp.concatenate([small] + [pltpu.roll(small, LANES - j * QUARTER, 1) for j in range(1, tiles)], axis=0)
    return gram, small, peak


def half_kernel(message, gram_ref, small_ref, peak_ref):
    gram_ref[...], small_ref[...], peak = sums_of(message)
    peak_ref[...] = jnp.broadcast_to(peak, peak_ref.shape)


def half_sums(message):
    rank = (message.shape[1] - 1) * TILE
    shape = jax.ShapeDtypeStruct((rank, LANES), jnp.float32)
    return pl.pallas_call(
        half_kernel,
        out_shape=(shape, shape, jax.ShapeDtypeStruct((8, LANES), jnp.float32)),
        in_specs=[VMEM],
        out_specs=(VMEM, VMEM, VMEM),
        compiler_params=pltpu.CompilerParams(vmem_limit_bytes=VMEM_LIMIT),
        cost_estimate=pl.CostEstimate(flops=message.size * rank, bytes_accessed=4 * message.size, transcendentals=0),
        name="half_sums",
    )(message)


def solve(own, got, replicas):
    shape = own[0].shape
    rank = shape[0]
    gram = own[0] + got[0]
    peak = jnp.maximum(own[2], got[2])
    small = own[1] * (own[2] / peak) + got[1] * (got[2] / peak)
    row = lax.broadcasted_iota(jnp.int32, shape, 0)
    column = [jnp.broadcast_to(gram[:, j : j + 1], shape) for j in range(rank)]
    trace = column[0][:1]
    for j in range(1, rank):
        trace = trace + column[j][j : j + 1]
    ridge = 1e-06 * trace / rank
    column = [jnp.where(row == j, column[j] + ridge, column[j]) for j in range(rank)]
    root = jnp.zeros(shape, jnp.float32)
    for k in range(rank):
        pivot = column[k][k : k + 1]
        inverse = 1.0 / pivot
        root = jnp.where(row == k, jnp.sqrt(inverse), root)
        factor = jnp.where(row > k, column[k] * inverse, 0.0)
        for j in range(k + 1, rank):
            column[j] = column[j] - factor * column[j][k : k + 1]
        small = small - factor * small[k : k + 1]
    new_q = small * (peak * root * (1.0 / replicas))
    coef = new_q * root
    for k in range(rank - 1, 0, -1):
        upper = jnp.where(row < k, column[k] * root * root, 0.0)
        coef = coef - upper * coef[k : k + 1]
    return new_q, coef


def finish_kernel(replicas, core_ref, own, got, gram, small, peak, mine, other, update, residual, new_q_ref,
                  update_buf, residual_buf, sems):
    chips, cols = mine.shape[:2]
    span = chips * LANES
    pieces = sems.shape[2]
    width = span // pieces
    starts = [pl.multiple_of(core_ref[0] * span, LANES), pl.multiple_of((1 - core_ref[0]) * span, LANES)]
    new_q, coef = solve((gram[...], small[...], peak[:1]), sums_of(got), replicas)
    new_q_ref[...] = new_q[:, :cols]
    first, second, third = split3(coef)
    lhs = jnp.concatenate([first, first, second, first, second, third], axis=0)
    lhs = jnp.transpose(lhs.astype(jnp.float32))[:cols].astype(jnp.bfloat16)
    stores = []
    for h, (source, merged) in enumerate(((own, mine), (got, other))):
        for i in range(0, chips, 2):
            left = jnp.concatenate([left_of(source, i), left_of(source, i + 1)], axis=1)
            one, two, three = split3(left)
            rhs = jnp.concatenate([one, two, one, three, two, one], axis=0)
            approx = jnp.dot(lhs, rhs, preferred_element_type=jnp.float32)
            at = slice(i * LANES, (i + 2) * LANES)
            update_buf[h, :, at] = approx.astype(jnp.bfloat16)
            residual_buf[h, :, at] = jnp.concatenate([merged[i], merged[i + 1]], axis=1) - approx
            done = (i + 2) * LANES
            if done % width == 0:
                piece = done // width - 1
                here = pl.ds(piece * width, width)
                there = pl.ds(pl.multiple_of(starts[h] + piece * width, LANES), width)
                one = pltpu.make_async_copy(update_buf.at[h, :, here], update.at[:, there], sems.at[0, h, piece])
                two = pltpu.make_async_copy(residual_buf.at[h, :, here], residual.at[:, there], sems.at[1, h, piece])
                one.start()
                two.start()
                stores += [one, two]
    for copy in stores:
        copy.wait()


def finish(core, own, got, sums, mine, other, replicas):
    chips, cols = mine.shape[:2]
    rank = sums[0].shape[0]
    span = chips * LANES
    pieces = 2
    return pl.pallas_call(
        functools.partial(finish_kernel, replicas),
        out_shape=(
            jax.ShapeDtypeStruct((cols, 2 * span), jnp.bfloat16),
            jax.ShapeDtypeStruct((cols, 2 * span), jnp.float32),
            jax.ShapeDtypeStruct((rank, cols), jnp.float32),
        ),
        in_specs=[SMEM] + [VMEM] * 7,
        out_specs=(ANY, ANY, VMEM),
        scratch_shapes=[
            pltpu.VMEM((2, cols, span), jnp.bfloat16),
            pltpu.VMEM((2, cols, span), jnp.float32),
            pltpu.SemaphoreType.DMA((2, 2, pieces)),
        ],
        compiler_params=pltpu.CompilerParams(vmem_limit_bytes=VMEM_LIMIT),
        name="finish",
    )(core.reshape(1), own, got, *sums, mine, other)


def per_device(grads, error, q_init):
    replicas = lax.axis_size("dp")
    shards = lax.axis_size("tensor")
    chips = replicas // 2
    rank = q_init.shape[1]
    grads, error = grads[0], error[0]
    core = lax.axis_index("dp") % 2
    other = merged_half(1 - core, grads, error)
    swapped = swap_cores(other)
    mine = merged_half(core, grads, error)
    total = across_chips(mine + swapped).sum(0)
    part = jnp.dot(q_init.T, total, precision=HIGHEST)
    order = list(range(0, shards, 2)) + list(range(1, shards, 2))
    parts = lax.all_to_all(jnp.broadcast_to(part, (shards, rank, LANES)), "tensor", 0, 0, axis_index_groups=[order])
    own = across_chips(message_of(parts, total, chips))
    got = swap_cores(own)
    update, residual, new_q = finish(core, own, got, half_sums(own), mine, other, replicas)
    return update, residual[None], new_q.T


def solution(mesh):
    in_specs = (P("dp", "tensor", None), P("dp", "tensor", None), P("tensor", None))
    out_specs = (P("tensor", None), P("dp", "tensor", None), P("tensor", None))
    return jax.shard_map(
        per_device, mesh=mesh, in_specs=in_specs, out_specs=out_specs, check_vma=False
    )
```

```python
import functools

import jax
import jax.numpy as jnp
from jax import lax
from jax.experimental import pallas as pl
from jax.experimental.pallas import tpu as pltpu
from jax.sharding import PartitionSpec as P

HIGHEST = lax.Precision.HIGHEST
LANES = 128
QUARTER = LANES // 4
TILE = 4
VMEM = pl.BlockSpec(memory_space=pltpu.VMEM)
SMEM = pl.BlockSpec(memory_space=pltpu.SMEM)
ANY = pl.BlockSpec(memory_space=pl.ANY)
HBM = pl.BlockSpec(memory_space=pltpu.HBM)
VMEM_LIMIT = 12 * 2**20


def swap_cores(value):
    count = lax.axis_size("dp")
    return lax.ppermute(value, "dp", [(i, i ^ 1) for i in range(count)])


def across_chips(value):
    count = lax.axis_size("dp")
    groups = [list(range(core, count, 2))[::-1] for core in range(2)]
    return lax.all_to_all(value, "dp", 0, 0, axis_index_groups=groups)


def merge_kernel(half_ref, grads, error, out, grad_buf, error_buf, sems):
    chips = out.shape[0]
    pieces = grad_buf.shape[0]
    width = grad_buf.shape[2]
    start = half_ref[0] * (chips * LANES)
    copies = []
    for i in range(pieces):
        at = pl.ds(pl.multiple_of(start + i * width, LANES), width)
        one = pltpu.make_async_copy(grads.at[:, at], grad_buf.at[i], sems.at[0, i])
        two = pltpu.make_async_copy(error.at[:, at], error_buf.at[i], sems.at[1, i])
        one.start()
        two.start()
        copies.append((one, two))
    for i in range(pieces):
        for copy in copies[i]:
            copy.wait()
        for j in range(width // LANES):
            at = slice(j * LANES, (j + 1) * LANES)
            out[i * (width // LANES) + j] = grad_buf[i, :, at].astype(jnp.float32) + error_buf[i, :, at]


def merged_half(half, grads, error):
    cols, depth = grads.shape
    chips = depth // (2 * LANES)
    pieces = 2
    width = depth // 2 // pieces
    return pl.pallas_call(
        merge_kernel,
        out_shape=jax.ShapeDtypeStruct((chips, cols, LANES), jnp.float32),
        in_specs=[SMEM, HBM, HBM],
        out_specs=VMEM,
        scratch_shapes=[
            pltpu.VMEM((pieces, cols, width), grads.dtype),
            pltpu.VMEM((pieces, cols, width), jnp.float32),
            pltpu.SemaphoreType.DMA((2, pieces)),
        ],
        compiler_params=pltpu.CompilerParams(vmem_limit_bytes=VMEM_LIMIT),
        cost_estimate=pl.CostEstimate(flops=cols * depth, bytes_accessed=5 * cols * depth, transcendentals=0),
        name="merge",
    )(half.reshape(1), *(pltpu.with_memory_space_constraint(x, pltpu.HBM) for x in (grads, error)))


def message_kernel(parts, total, out):
    chips, tiles = out.shape[:2]
    left = parts[0]
    for i in range(1, parts.shape[0]):
        left = left + parts[i]
    scaled = left / peak_of(left)
    pad = jnp.zeros((LANES - total.shape[0], LANES), jnp.float32)
    other = jnp.concatenate([total[...], pad], axis=0)
    small = lax.dot_general(scaled, other, (((1,), (1,)), ((), ())), precision=HIGHEST, preferred_element_type=jnp.float32)
    lane = lax.broadcasted_iota(jnp.int32, (TILE, LANES), 1)
    packed = small[:TILE]
    for j in range(1, tiles - 1):
        piece = pltpu.roll(small, j * QUARTER, 1)[j * TILE : (j + 1) * TILE]
        packed = jnp.where(lane >= j * QUARTER, piece, packed)
    pieces = [left[j * TILE : (j + 1) * TILE] for j in range(tiles - 1)] + [packed]
    for i in range(chips):
        for j in range(tiles):
            out[i, j] = pieces[j]


def message_of(parts, total, chips):
    tiles = parts.shape[1] // TILE + 1
    return pl.pallas_call(
        message_kernel,
        out_shape=jax.ShapeDtypeStruct((chips, tiles, TILE, LANES), jnp.float32),
        in_specs=[VMEM, VMEM],
        out_specs=VMEM,
        compiler_params=pltpu.CompilerParams(vmem_limit_bytes=VMEM_LIMIT),
        name="message",
    )(parts, total)


def peak_of(left):
    peak = jnp.max(jnp.max(jnp.abs(left), axis=1, keepdims=True), axis=0, keepdims=True)
    return jnp.maximum(peak, 1e-30)


def split3(value):
    first = value.astype(jnp.bfloat16)
    rest = value - first.astype(jnp.float32)
    second = rest.astype(jnp.bfloat16)
    third = (rest - second.astype(jnp.float32)).astype(jnp.bfloat16)
    return first, second, third


def left_of(message, i):
    tiles = message.shape[1] - 1
    return jnp.concatenate([message[i, j] for j in range(tiles)], axis=0)


def sums_of(message):
    chips, tiles = message.shape[0], message.shape[1] - 1
    rank = tiles * TILE
    square = jnp.zeros((3 * rank, 3 * rank), jnp.float32)
    peaks = []
    for i in range(0, chips, 2):
        pair = [left_of(message, i), left_of(message, i + 1)]
        peaks += [jnp.broadcast_to(peak_of(left), (1, LANES)) for left in pair]
        terms = jnp.concatenate(split3(jnp.concatenate(pair, axis=1)), axis=0)
        square += lax.dot_general(terms, terms, (((1,), (1,)), ((), ())), preferred_element_type=jnp.float32)
    at = [slice(i * rank, (i + 1) * rank) for i in range(3)]
    cross = square[at[0], at[2]] + square[at[2], at[0]] + square[at[1], at[1]]
    cross = cross + (square[at[0], at[1]] + square[at[1], at[0]])
    gram = square[at[0], at[0]] + cross
    gram = jnp.concatenate([gram, jnp.zeros((rank, LANES - rank), jnp.float32)], axis=1)
    peak = functools.reduce(jnp.maximum, peaks)
    inverse = 1.0 / peak
    small = functools.reduce(jnp.add, [message[i, tiles] * (peaks[i] * inverse) for i in range(chips)])
    small = jnp.concatenate([small] + [pltpu.roll(small, LANES - j * QUARTER, 1) for j in range(1, tiles)], axis=0)
    return gram, small, peak


def half_kernel(message, gram_ref, small_ref, peak_ref):
    gram_ref[...], small_ref[...], peak = sums_of(message)
    peak_ref[...] = jnp.broadcast_to(peak, peak_ref.shape)


def half_sums(message):
    rank = (message.shape[1] - 1) * TILE
    shape = jax.ShapeDtypeStruct((rank, LANES), jnp.float32)
    return pl.pallas_call(
        half_kernel,
        out_shape=(shape, shape, jax.ShapeDtypeStruct((8, LANES), jnp.float32)),
        in_specs=[VMEM],
        out_specs=(VMEM, VMEM, VMEM),
        compiler_params=pltpu.CompilerParams(vmem_limit_bytes=VMEM_LIMIT),
        cost_estimate=pl.CostEstimate(flops=message.size * rank, bytes_accessed=4 * message.size, transcendentals=0),
        name="half_sums",
    )(message)


def solve(own, got, replicas):
    shape = own[0].shape
    rank = shape[0]
    gram = own[0] + got[0]
    peak = jnp.maximum(own[2], got[2])
    small = own[1] * (own[2] / peak) + got[1] * (got[2] / peak)
    row = lax.broadcasted_iota(jnp.int32, shape, 0)
    column = [jnp.broadcast_to(gram[:, j : j + 1], shape) for j in range(rank)]
    trace = column[0][:1]
    for j in range(1, rank):
        trace = trace + column[j][j : j + 1]
    ridge = 1e-06 * trace / rank
    column = [jnp.where(row == j, column[j] + ridge, column[j]) for j in range(rank)]
    root = jnp.zeros(shape, jnp.float32)
    for k in range(rank):
        pivot = column[k][k : k + 1]
        inverse = 1.0 / pivot
        root = jnp.where(row == k, jnp.sqrt(inverse), root)
        factor = jnp.where(row > k, column[k] * inverse, 0.0)
        for j in range(k + 1, rank):
            column[j] = column[j] - factor * column[j][k : k + 1]
        small = small - factor * small[k : k + 1]
    new_q = small * (peak * root * (1.0 / replicas))
    coef = new_q * root
    for k in range(rank - 1, 0, -1):
        upper = jnp.where(row < k, column[k] * root * root, 0.0)
        coef = coef - upper * coef[k : k + 1]
    return new_q, coef


def finish_kernel(replicas, core_ref, own, got, gram, small, peak, mine, other, update, residual, new_q_ref,
                  update_buf, residual_buf, sems):
    chips, cols = mine.shape[:2]
    span = chips * LANES
    pieces = sems.shape[2]
    width = span // pieces
    starts = [pl.multiple_of(core_ref[0] * span, LANES), pl.multiple_of((1 - core_ref[0]) * span, LANES)]
    new_q, coef = solve((gram[...], small[...], peak[:1]), sums_of(got), replicas)
    new_q_ref[...] = new_q[:, :cols]
    first, second, third = split3(coef)
    lhs = jnp.concatenate([first, first, second, first, second, third], axis=0)
    lhs = jnp.transpose(lhs.astype(jnp.float32))[:cols].astype(jnp.bfloat16)
    stores = []
    for h, (source, merged) in enumerate(((own, mine), (got, other))):
        for i in range(0, chips, 2):
            left = jnp.concatenate([left_of(source, i), left_of(source, i + 1)], axis=1)
            one, two, three = split3(left)
            rhs = jnp.concatenate([one, two, one, three, two, one], axis=0)
            approx = jnp.dot(lhs, rhs, preferred_element_type=jnp.float32)
            at = slice(i * LANES, (i + 2) * LANES)
            update_buf[h, :, at] = approx.astype(jnp.bfloat16)
            residual_buf[h, :, at] = jnp.concatenate([merged[i], merged[i + 1]], axis=1) - approx
            done = (i + 2) * LANES
            if done % width == 0:
                piece = done // width - 1
                here = pl.ds(piece * width, width)
                there = pl.ds(pl.multiple_of(starts[h] + piece * width, LANES), width)
                one = pltpu.make_async_copy(update_buf.at[h, :, here], update.at[:, there], sems.at[0, h, piece])
                two = pltpu.make_async_copy(residual_buf.at[h, :, here], residual.at[:, there], sems.at[1, h, piece])
                one.start()
                two.start()
                stores += [one, two]
    for copy in stores:
        copy.wait()


def finish(core, own, got, sums, mine, other, replicas):
    chips, cols = mine.shape[:2]
    rank = sums[0].shape[0]
    span = chips * LANES
    pieces = 2
    return pl.pallas_call(
        functools.partial(finish_kernel, replicas),
        out_shape=(
            jax.ShapeDtypeStruct((cols, 2 * span), jnp.bfloat16),
            jax.ShapeDtypeStruct((cols, 2 * span), jnp.float32),
            jax.ShapeDtypeStruct((rank, cols), jnp.float32),
        ),
        in_specs=[SMEM] + [VMEM] * 7,
        out_specs=(ANY, ANY, VMEM),
        scratch_shapes=[
            pltpu.VMEM((2, cols, span), jnp.bfloat16),
            pltpu.VMEM((2, cols, span), jnp.float32),
            pltpu.SemaphoreType.DMA((2, 2, pieces)),
        ],
        compiler_params=pltpu.CompilerParams(vmem_limit_bytes=VMEM_LIMIT),
        name="finish",
    )(core.reshape(1), own, got, *sums, mine, other)


def per_device(grads, error, q_init):
    replicas = lax.axis_size("dp")
    shards = lax.axis_size("tensor")
    chips = replicas // 2
    rank = q_init.shape[1]
    grads, error = grads[0], error[0]
    core = lax.axis_index("dp") % 2
    other = merged_half(1 - core, grads, error)
    swapped = swap_cores(other)
    mine = merged_half(core, grads, error)
    total = across_chips(mine + swapped).sum(0)
    part = jnp.dot(q_init.T, total, precision=HIGHEST)
    order = sorted(range(shards), key=lambda i: (min(i, shards - i), i > shards // 2))[::-1]
    parts = lax.all_to_all(jnp.broadcast_to(part, (shards, rank, LANES)), "tensor", 0, 0, axis_index_groups=[order])
    own = across_chips(message_of(parts, total, chips))
    got = swap_cores(own)
    update, residual, new_q = finish(core, own, got, half_sums(own), mine, other, replicas)
    return update, residual[None], new_q.T


def solution(mesh):
    in_specs = (P("dp", "tensor", None), P("dp", "tensor", None), P("tensor", None))
    out_specs = (P("tensor", None), P("dp", "tensor", None), P("tensor", None))
    return jax.shard_map(
        per_device, mesh=mesh, in_specs=in_specs, out_specs=out_specs, check_vma=False
    )
```

```python
import functools

import jax
import jax.numpy as jnp
from jax import lax
from jax.experimental import pallas as pl
from jax.experimental.pallas import tpu as pltpu
from jax.sharding import PartitionSpec as P

HIGHEST = lax.Precision.HIGHEST
LANES = 128
QUARTER = LANES // 4
TILE = 4
VMEM = pl.BlockSpec(memory_space=pltpu.VMEM)
SMEM = pl.BlockSpec(memory_space=pltpu.SMEM)
ANY = pl.BlockSpec(memory_space=pl.ANY)
HBM = pl.BlockSpec(memory_space=pltpu.HBM)
VMEM_LIMIT = 12 * 2**20


def swap_cores(value):
    count = lax.axis_size("dp")
    return lax.ppermute(value, "dp", [(i, i ^ 1) for i in range(count)])


def across_chips(value):
    count = lax.axis_size("dp")
    groups = [list(range(core, count, 2))[::-1] for core in range(2)]
    return lax.all_to_all(value, "dp", 0, 0, axis_index_groups=groups)


def merge_kernel(half_ref, grads, error, out, grad_buf, error_buf, sems):
    chips = out.shape[0]
    pieces = grad_buf.shape[0]
    width = grad_buf.shape[2]
    start = half_ref[0] * (chips * LANES)
    copies = []
    for i in range(pieces):
        at = pl.ds(pl.multiple_of(start + i * width, LANES), width)
        one = pltpu.make_async_copy(grads.at[:, at], grad_buf.at[i], sems.at[0, i])
        two = pltpu.make_async_copy(error.at[:, at], error_buf.at[i], sems.at[1, i])
        one.start()
        two.start()
        copies.append((one, two))
    for i in range(pieces):
        for copy in copies[i]:
            copy.wait()
        for j in range(width // LANES):
            at = slice(j * LANES, (j + 1) * LANES)
            out[i * (width // LANES) + j] = grad_buf[i, :, at].astype(jnp.float32) + error_buf[i, :, at]


def merged_half(half, grads, error):
    cols, depth = grads.shape
    chips = depth // (2 * LANES)
    pieces = 2
    width = depth // 2 // pieces
    return pl.pallas_call(
        merge_kernel,
        out_shape=jax.ShapeDtypeStruct((chips, cols, LANES), jnp.float32),
        in_specs=[SMEM, HBM, HBM],
        out_specs=VMEM,
        scratch_shapes=[
            pltpu.VMEM((pieces, cols, width), grads.dtype),
            pltpu.VMEM((pieces, cols, width), jnp.float32),
            pltpu.SemaphoreType.DMA((2, pieces)),
        ],
        compiler_params=pltpu.CompilerParams(vmem_limit_bytes=VMEM_LIMIT),
        cost_estimate=pl.CostEstimate(flops=cols * depth, bytes_accessed=5 * cols * depth, transcendentals=0),
        name="merge",
    )(half.reshape(1), *(pltpu.with_memory_space_constraint(x, pltpu.HBM) for x in (grads, error)))


def message_kernel(parts, total, out):
    chips, tiles = out.shape[:2]
    left = parts[0]
    for i in range(1, parts.shape[0]):
        left = left + parts[i]
    scaled = left / peak_of(left)
    pad = jnp.zeros((LANES - total.shape[0], LANES), jnp.float32)
    other = jnp.concatenate([total[...], pad], axis=0)
    small = lax.dot_general(scaled, other, (((1,), (1,)), ((), ())), precision=HIGHEST, preferred_element_type=jnp.float32)
    lane = lax.broadcasted_iota(jnp.int32, (TILE, LANES), 1)
    packed = small[:TILE]
    for j in range(1, tiles - 1):
        piece = pltpu.roll(small, j * QUARTER, 1)[j * TILE : (j + 1) * TILE]
        packed = jnp.where(lane >= j * QUARTER, piece, packed)
    pieces = [left[j * TILE : (j + 1) * TILE] for j in range(tiles - 1)] + [packed]
    for i in range(chips):
        for j in range(tiles):
            out[i, j] = pieces[j]


def message_of(parts, total, chips):
    tiles = parts.shape[1] // TILE + 1
    return pl.pallas_call(
        message_kernel,
        out_shape=jax.ShapeDtypeStruct((chips, tiles, TILE, LANES), jnp.float32),
        in_specs=[VMEM, VMEM],
        out_specs=VMEM,
        compiler_params=pltpu.CompilerParams(vmem_limit_bytes=VMEM_LIMIT),
        name="message",
    )(parts, total)


def peak_of(left):
    peak = jnp.max(jnp.max(jnp.abs(left), axis=1, keepdims=True), axis=0, keepdims=True)
    return jnp.maximum(peak, 1e-30) * 128.0


def split3(value):
    first = value.astype(jnp.bfloat16)
    rest = value - first.astype(jnp.float32)
    second = rest.astype(jnp.bfloat16)
    third = (rest - second.astype(jnp.float32)).astype(jnp.bfloat16)
    return first, second, third


def left_of(message, i):
    tiles = message.shape[1] - 1
    return jnp.concatenate([message[i, j] for j in range(tiles)], axis=0)


def sums_of(message):
    chips, tiles = message.shape[0], message.shape[1] - 1
    rank = tiles * TILE
    square = jnp.zeros((3 * rank, 3 * rank), jnp.float32)
    peaks = []
    for i in range(0, chips, 2):
        pair = [left_of(message, i), left_of(message, i + 1)]
        peaks += [jnp.broadcast_to(peak_of(left), (1, LANES)) for left in pair]
        terms = jnp.concatenate(split3(jnp.concatenate(pair, axis=1)), axis=0)
        square += lax.dot_general(terms, terms, (((1,), (1,)), ((), ())), preferred_element_type=jnp.float32)
    at = [slice(i * rank, (i + 1) * rank) for i in range(3)]
    cross = square[at[0], at[2]] + square[at[2], at[0]] + square[at[1], at[1]]
    cross = cross + (square[at[0], at[1]] + square[at[1], at[0]])
    gram = square[at[0], at[0]] + cross
    gram = jnp.concatenate([gram, jnp.zeros((rank, LANES - rank), jnp.float32)], axis=1)
    peak = functools.reduce(jnp.maximum, peaks)
    inverse = 1.0 / peak
    small = functools.reduce(jnp.add, [message[i, tiles] * (peaks[i] * inverse) for i in range(chips)])
    small = jnp.concatenate([small] + [pltpu.roll(small, LANES - j * QUARTER, 1) for j in range(1, tiles)], axis=0)
    return gram, small, peak


def half_kernel(message, gram_ref, small_ref, peak_ref):
    gram_ref[...], small_ref[...], peak = sums_of(message)
    peak_ref[...] = jnp.broadcast_to(peak, peak_ref.shape)


def half_sums(message):
    rank = (message.shape[1] - 1) * TILE
    shape = jax.ShapeDtypeStruct((rank, LANES), jnp.float32)
    return pl.pallas_call(
        half_kernel,
        out_shape=(shape, shape, jax.ShapeDtypeStruct((8, LANES), jnp.float32)),
        in_specs=[VMEM],
        out_specs=(VMEM, VMEM, VMEM),
        compiler_params=pltpu.CompilerParams(vmem_limit_bytes=VMEM_LIMIT),
        cost_estimate=pl.CostEstimate(flops=message.size * rank, bytes_accessed=4 * message.size, transcendentals=0),
        name="half_sums",
    )(message)


def solve(own, got, replicas):
    shape = own[0].shape
    rank = shape[0]
    gram = own[0] + got[0]
    peak = jnp.maximum(own[2], got[2])
    small = own[1] * (own[2] / peak) + got[1] * (got[2] / peak)
    row = lax.broadcasted_iota(jnp.int32, shape, 0)
    column = [jnp.broadcast_to(gram[:, j : j + 1], shape) for j in range(rank)]
    trace = column[0][:1]
    for j in range(1, rank):
        trace = trace + column[j][j : j + 1]
    ridge = 1e-06 * trace / rank
    column = [jnp.where(row == j, column[j] + ridge, column[j]) for j in range(rank)]
    root = jnp.zeros(shape, jnp.float32)
    for k in range(rank):
        pivot = column[k][k : k + 1]
        inverse = lax.rsqrt(pivot)
        root = jnp.where(row == k, inverse, root)
        factor = jnp.where(row > k, column[k] * inverse * inverse, 0.0)
        for j in range(k + 1, rank):
            column[j] = column[j] - factor * column[j][k : k + 1]
        small = small - factor * small[k : k + 1]
    scale = peak * root
    new_q = small * (scale * (1.0 / replicas))
    coef = new_q * scale
    for k in range(rank - 1, 0, -1):
        upper = jnp.where(row < k, column[k] * root * root, 0.0)
        coef = coef - upper * coef[k : k + 1]
    return new_q, coef, 1.0 / peak


def finish_kernel(replicas, core_ref, own, got, gram, small, peak, mine, other, update, residual, new_q_ref,
                  update_buf, residual_buf, sems):
    chips, cols = mine.shape[:2]
    span = chips * LANES
    pieces = sems.shape[2]
    width = span // pieces
    starts = [pl.multiple_of(core_ref[0] * span, LANES), pl.multiple_of((1 - core_ref[0]) * span, LANES)]
    new_q, coef, inverse = solve((gram[...], small[...], peak[:1]), sums_of(got), replicas)
    new_q_ref[...] = new_q[:, :cols]
    first, second, third = split3(coef)
    lhs = jnp.concatenate([first, first, second, first, second, third], axis=0)
    lhs = jnp.transpose(lhs.astype(jnp.float32))[:cols].astype(jnp.bfloat16)
    stores = []
    for h, (source, merged) in enumerate(((own, mine), (got, other))):
        for i in range(0, chips, 2):
            left = jnp.concatenate([left_of(source, i) * inverse, left_of(source, i + 1) * inverse], axis=1)
            one, two, three = split3(left)
            rhs = jnp.concatenate([one, two, one, three, two, one], axis=0)
            approx = jnp.dot(lhs, rhs, preferred_element_type=jnp.float32)
            at = slice(i * LANES, (i + 2) * LANES)
            update_buf[h, :, at] = approx.astype(jnp.bfloat16)
            residual_buf[h, :, at] = jnp.concatenate([merged[i], merged[i + 1]], axis=1) - approx
            done = (i + 2) * LANES
            if done % width == 0:
                piece = done // width - 1
                here = pl.ds(piece * width, width)
                there = pl.ds(pl.multiple_of(starts[h] + piece * width, LANES), width)
                one = pltpu.make_async_copy(update_buf.at[h, :, here], update.at[:, there], sems.at[0, h, piece])
                two = pltpu.make_async_copy(residual_buf.at[h, :, here], residual.at[:, there], sems.at[1, h, piece])
                one.start()
                two.start()
                stores += [one, two]
    for copy in stores:
        copy.wait()


def finish(core, own, got, sums, mine, other, replicas):
    chips, cols = mine.shape[:2]
    rank = sums[0].shape[0]
    span = chips * LANES
    pieces = 2
    return pl.pallas_call(
        functools.partial(finish_kernel, replicas),
        out_shape=(
            jax.ShapeDtypeStruct((cols, 2 * span), jnp.bfloat16),
            jax.ShapeDtypeStruct((cols, 2 * span), jnp.float32),
            jax.ShapeDtypeStruct((rank, cols), jnp.float32),
        ),
        in_specs=[SMEM] + [VMEM] * 7,
        out_specs=(ANY, ANY, VMEM),
        scratch_shapes=[
            pltpu.VMEM((2, cols, span), jnp.bfloat16),
            pltpu.VMEM((2, cols, span), jnp.float32),
            pltpu.SemaphoreType.DMA((2, 2, pieces)),
        ],
        compiler_params=pltpu.CompilerParams(vmem_limit_bytes=VMEM_LIMIT),
        name="finish",
    )(core.reshape(1), own, got, *sums, mine, other)


def per_device(grads, error, q_init):
    replicas = lax.axis_size("dp")
    shards = lax.axis_size("tensor")
    chips = replicas // 2
    rank = q_init.shape[1]
    grads, error = grads[0], error[0]
    core = lax.axis_index("dp") % 2
    other = merged_half(1 - core, grads, error)
    swapped = swap_cores(other)
    mine = merged_half(core, grads, error)
    total = across_chips(mine + swapped).sum(0)
    part = jnp.dot(q_init.T, total, precision=HIGHEST)
    order = sorted(range(shards), key=lambda i: (min(i, shards - i), i > shards // 2))[::-1]
    parts = lax.all_to_all(jnp.broadcast_to(part, (shards, rank, LANES)), "tensor", 0, 0, axis_index_groups=[order])
    own = across_chips(message_of(parts, total, chips))
    got = swap_cores(own)
    update, residual, new_q = finish(core, own, got, half_sums(own), mine, other, replicas)
    return update, residual[None], new_q.T


def solution(mesh):
    in_specs = (P("dp", "tensor", None), P("dp", "tensor", None), P("tensor", None))
    out_specs = (P("tensor", None), P("dp", "tensor", None), P("tensor", None))
    return jax.shard_map(
        per_device, mesh=mesh, in_specs=in_specs, out_specs=out_specs, check_vma=False
    )
```

```python
import functools

import jax
import jax.numpy as jnp
from jax import lax
from jax.experimental import pallas as pl
from jax.experimental.pallas import tpu as pltpu
from jax.sharding import PartitionSpec as P

HIGHEST = lax.Precision.HIGHEST
LANES = 128
QUARTER = LANES // 4
TILE = 4
VMEM = pl.BlockSpec(memory_space=pltpu.VMEM)
SMEM = pl.BlockSpec(memory_space=pltpu.SMEM)
ANY = pl.BlockSpec(memory_space=pl.ANY)
HBM = pl.BlockSpec(memory_space=pltpu.HBM)
VMEM_LIMIT = 12 * 2**20
X_ORDER = (2, 3, 1, 0)
TENSOR_ORDER = (4, 5, 6, 3, 2, 7, 1, 0)


def swap_cores(value):
    count = lax.axis_size("dp")
    return lax.ppermute(value, "dp", [(i, i ^ 1) for i in range(count)])


def across_chips(value):
    rows = lax.axis_size("dp") // (2 * len(X_ORDER))
    chips = [z * len(X_ORDER) + x for z in reversed(range(rows)) for x in X_ORDER]
    groups = [[2 * chip + core for chip in chips] for core in range(2)]
    return lax.all_to_all(value, "dp", 0, 0, axis_index_groups=groups)


def merge_kernel(half_ref, grads, error, out, grad_buf, error_buf, sems):
    chips = out.shape[0]
    pieces = grad_buf.shape[0]
    width = grad_buf.shape[2]
    start = half_ref[0] * (chips * LANES)
    copies = []
    for i in range(pieces):
        at = pl.ds(pl.multiple_of(start + i * width, LANES), width)
        one = pltpu.make_async_copy(grads.at[:, at], grad_buf.at[i], sems.at[0, i])
        two = pltpu.make_async_copy(error.at[:, at], error_buf.at[i], sems.at[1, i])
        one.start()
        two.start()
        copies.append((one, two))
    for i in range(pieces):
        for copy in copies[i]:
            copy.wait()
        for j in range(width // LANES):
            at = slice(j * LANES, (j + 1) * LANES)
            out[i * (width // LANES) + j] = grad_buf[i, :, at].astype(jnp.float32) + error_buf[i, :, at]


def merged_half(half, grads, error):
    cols, depth = grads.shape
    chips = depth // (2 * LANES)
    pieces = 2
    width = depth // 2 // pieces
    return pl.pallas_call(
        merge_kernel,
        out_shape=jax.ShapeDtypeStruct((chips, cols, LANES), jnp.float32),
        in_specs=[SMEM, HBM, HBM],
        out_specs=VMEM,
        scratch_shapes=[
            pltpu.VMEM((pieces, cols, width), grads.dtype),
            pltpu.VMEM((pieces, cols, width), jnp.float32),
            pltpu.SemaphoreType.DMA((2, pieces)),
        ],
        compiler_params=pltpu.CompilerParams(vmem_limit_bytes=VMEM_LIMIT),
        cost_estimate=pl.CostEstimate(flops=cols * depth, bytes_accessed=5 * cols * depth, transcendentals=0),
        name="merge",
    )(half.reshape(1), *(pltpu.with_memory_space_constraint(x, pltpu.HBM) for x in (grads, error)))


def message_kernel(parts, total, out):
    chips, tiles = out.shape[:2]
    left = parts[0]
    for i in range(1, parts.shape[0]):
        left = left + parts[i]
    scaled = left / peak_of(left)
    pad = jnp.zeros((LANES - total.shape[0], LANES), jnp.float32)
    other = jnp.concatenate([total[...], pad], axis=0)
    small = lax.dot_general(scaled, other, (((1,), (1,)), ((), ())), precision=HIGHEST, preferred_element_type=jnp.float32)
    lane = lax.broadcasted_iota(jnp.int32, (TILE, LANES), 1)
    packed = small[:TILE]
    for j in range(1, tiles - 1):
        piece = pltpu.roll(small, j * QUARTER, 1)[j * TILE : (j + 1) * TILE]
        packed = jnp.where(lane >= j * QUARTER, piece, packed)
    pieces = [left[j * TILE : (j + 1) * TILE] for j in range(tiles - 1)] + [packed]
    for i in range(chips):
        for j in range(tiles):
            out[i, j] = pieces[j]


def message_of(parts, total, chips):
    tiles = parts.shape[1] // TILE + 1
    return pl.pallas_call(
        message_kernel,
        out_shape=jax.ShapeDtypeStruct((chips, tiles, TILE, LANES), jnp.float32),
        in_specs=[VMEM, VMEM],
        out_specs=VMEM,
        compiler_params=pltpu.CompilerParams(vmem_limit_bytes=VMEM_LIMIT),
        name="message",
    )(parts, total)


def peak_of(left):
    peak = jnp.max(jnp.max(jnp.abs(left), axis=1, keepdims=True), axis=0, keepdims=True)
    return jnp.maximum(peak, 1e-30) * 128.0


def split3(value):
    first = value.astype(jnp.bfloat16)
    rest = value - first.astype(jnp.float32)
    second = rest.astype(jnp.bfloat16)
    third = (rest - second.astype(jnp.float32)).astype(jnp.bfloat16)
    return first, second, third


def left_of(message, i):
    tiles = message.shape[1] - 1
    return jnp.concatenate([message[i, j] for j in range(tiles)], axis=0)


def sums_of(message):
    chips, tiles = message.shape[0], message.shape[1] - 1
    rank = tiles * TILE
    square = jnp.zeros((3 * rank, 3 * rank), jnp.float32)
    peaks = []
    for i in range(0, chips, 2):
        pair = [left_of(message, i), left_of(message, i + 1)]
        peaks += [jnp.broadcast_to(peak_of(left), (1, LANES)) for left in pair]
        terms = jnp.concatenate(split3(jnp.concatenate(pair, axis=1)), axis=0)
        square += lax.dot_general(terms, terms, (((1,), (1,)), ((), ())), preferred_element_type=jnp.float32)
    at = [slice(i * rank, (i + 1) * rank) for i in range(3)]
    cross = square[at[0], at[2]] + square[at[2], at[0]] + square[at[1], at[1]]
    cross = cross + (square[at[0], at[1]] + square[at[1], at[0]])
    gram = square[at[0], at[0]] + cross
    gram = jnp.concatenate([gram, jnp.zeros((rank, LANES - rank), jnp.float32)], axis=1)
    peak = functools.reduce(jnp.maximum, peaks)
    inverse = 1.0 / peak
    small = functools.reduce(jnp.add, [message[i, tiles] * (peaks[i] * inverse) for i in range(chips)])
    small = jnp.concatenate([small] + [pltpu.roll(small, LANES - j * QUARTER, 1) for j in range(1, tiles)], axis=0)
    return gram, small, peak


def half_kernel(message, gram_ref, small_ref, peak_ref):
    gram_ref[...], small_ref[...], peak = sums_of(message)
    peak_ref[...] = jnp.broadcast_to(peak, peak_ref.shape)


def half_sums(message):
    rank = (message.shape[1] - 1) * TILE
    shape = jax.ShapeDtypeStruct((rank, LANES), jnp.float32)
    return pl.pallas_call(
        half_kernel,
        out_shape=(shape, shape, jax.ShapeDtypeStruct((8, LANES), jnp.float32)),
        in_specs=[VMEM],
        out_specs=(VMEM, VMEM, VMEM),
        compiler_params=pltpu.CompilerParams(vmem_limit_bytes=VMEM_LIMIT),
        cost_estimate=pl.CostEstimate(flops=message.size * rank, bytes_accessed=4 * message.size, transcendentals=0),
        name="half_sums",
    )(message)


def solve(own, got, replicas):
    shape = own[0].shape
    rank = shape[0]
    gram = own[0] + got[0]
    peak = jnp.maximum(own[2], got[2])
    small = own[1] * (own[2] / peak) + got[1] * (got[2] / peak)
    row = lax.broadcasted_iota(jnp.int32, shape, 0)
    column = [jnp.broadcast_to(gram[:, j : j + 1], shape) for j in range(rank)]
    trace = column[0][:1]
    for j in range(1, rank):
        trace = trace + column[j][j : j + 1]
    ridge = 1e-06 * trace / rank
    column = [jnp.where(row == j, column[j] + ridge, column[j]) for j in range(rank)]
    root = jnp.zeros(shape, jnp.float32)
    for k in range(rank):
        pivot = column[k][k : k + 1]
        inverse = lax.rsqrt(pivot)
        root = jnp.where(row == k, inverse, root)
        factor = jnp.where(row > k, column[k] * inverse * inverse, 0.0)
        for j in range(k + 1, rank):
            column[j] = column[j] - factor * column[j][k : k + 1]
        small = small - factor * small[k : k + 1]
    scale = peak * root
    new_q = small * (scale * (1.0 / replicas))
    coef = new_q * scale
    for k in range(rank - 1, 0, -1):
        upper = jnp.where(row < k, column[k] * root * root, 0.0)
        coef = coef - upper * coef[k : k + 1]
    return new_q, coef, 1.0 / peak


def finish_kernel(replicas, core_ref, own, got, gram, small, peak, mine, other, update, residual, new_q_ref,
                  update_buf, residual_buf, sems):
    chips, cols = mine.shape[:2]
    span = chips * LANES
    pieces = sems.shape[2]
    width = span // pieces
    starts = [pl.multiple_of(core_ref[0] * span, LANES), pl.multiple_of((1 - core_ref[0]) * span, LANES)]
    new_q, coef, inverse = solve((gram[...], small[...], peak[:1]), sums_of(got), replicas)
    new_q_ref[...] = new_q[:, :cols]
    first, second, third = split3(coef)
    lhs = jnp.concatenate([first, first, second, first, second, third], axis=0)
    lhs = jnp.transpose(lhs.astype(jnp.float32))[:cols].astype(jnp.bfloat16)
    stores = []
    for h, (source, merged) in enumerate(((own, mine), (got, other))):
        for i in range(0, chips, 2):
            left = jnp.concatenate([left_of(source, i) * inverse, left_of(source, i + 1) * inverse], axis=1)
            one, two, three = split3(left)
            rhs = jnp.concatenate([one, two, one, three, two, one], axis=0)
            approx = jnp.dot(lhs, rhs, preferred_element_type=jnp.float32)
            at = slice(i * LANES, (i + 2) * LANES)
            update_buf[h, :, at] = approx.astype(jnp.bfloat16)
            residual_buf[h, :, at] = jnp.concatenate([merged[i], merged[i + 1]], axis=1) - approx
            done = (i + 2) * LANES
            if done % width == 0:
                piece = done // width - 1
                here = pl.ds(piece * width, width)
                there = pl.ds(pl.multiple_of(starts[h] + piece * width, LANES), width)
                one = pltpu.make_async_copy(update_buf.at[h, :, here], update.at[:, there], sems.at[0, h, piece])
                two = pltpu.make_async_copy(residual_buf.at[h, :, here], residual.at[:, there], sems.at[1, h, piece])
                one.start()
                two.start()
                stores += [one, two]
    for copy in stores:
        copy.wait()


def finish(core, own, got, sums, mine, other, replicas):
    chips, cols = mine.shape[:2]
    rank = sums[0].shape[0]
    span = chips * LANES
    pieces = 2
    return pl.pallas_call(
        functools.partial(finish_kernel, replicas),
        out_shape=(
            jax.ShapeDtypeStruct((cols, 2 * span), jnp.bfloat16),
            jax.ShapeDtypeStruct((cols, 2 * span), jnp.float32),
            jax.ShapeDtypeStruct((rank, cols), jnp.float32),
        ),
        in_specs=[SMEM] + [VMEM] * 7,
        out_specs=(ANY, ANY, VMEM),
        scratch_shapes=[
            pltpu.VMEM((2, cols, span), jnp.bfloat16),
            pltpu.VMEM((2, cols, span), jnp.float32),
            pltpu.SemaphoreType.DMA((2, 2, pieces)),
        ],
        compiler_params=pltpu.CompilerParams(vmem_limit_bytes=VMEM_LIMIT),
        name="finish",
    )(core.reshape(1), own, got, *sums, mine, other)


def per_device(grads, error, q_init):
    replicas = lax.axis_size("dp")
    shards = lax.axis_size("tensor")
    chips = replicas // 2
    rank = q_init.shape[1]
    grads, error = grads[0], error[0]
    core = lax.axis_index("dp") % 2
    other = merged_half(1 - core, grads, error)
    swapped = swap_cores(other)
    mine = merged_half(core, grads, error)
    total = across_chips(mine + swapped).sum(0)
    part = jnp.dot(q_init.T, total, precision=HIGHEST)
    order = [i for i in TENSOR_ORDER if i < shards]
    parts = lax.all_to_all(jnp.broadcast_to(part, (shards, rank, LANES)), "tensor", 0, 0, axis_index_groups=[order])
    own = across_chips(message_of(parts, total, chips))
    got = swap_cores(own)
    update, residual, new_q = finish(core, own, got, half_sums(own), mine, other, replicas)
    return update, residual[None], new_q.T


def solution(mesh):
    in_specs = (P("dp", "tensor", None), P("dp", "tensor", None), P("tensor", None))
    out_specs = (P("tensor", None), P("dp", "tensor", None), P("tensor", None))
    return jax.shard_map(
        per_device, mesh=mesh, in_specs=in_specs, out_specs=out_specs, check_vma=False
    )
```

```python
import functools

import jax
import jax.numpy as jnp
from jax import lax
from jax.experimental import pallas as pl
from jax.experimental.pallas import tpu as pltpu
from jax.sharding import PartitionSpec as P

HIGHEST = lax.Precision.HIGHEST
LANES = 128
QUARTER = LANES // 4
TILE = 4
VMEM = pl.BlockSpec(memory_space=pltpu.VMEM)
SMEM = pl.BlockSpec(memory_space=pltpu.SMEM)
ANY = pl.BlockSpec(memory_space=pl.ANY)
HBM = pl.BlockSpec(memory_space=pltpu.HBM)
VMEM_LIMIT = 12 * 2**20
X_ORDER = (2, 3, 1, 0)
TENSOR_ORDER = (4, 5, 6, 3, 2, 7, 1, 0)


def swap_cores(value):
    count = lax.axis_size("dp")
    return lax.ppermute(value, "dp", [(i, i ^ 1) for i in range(count)])


def across_chips(value):
    rows = lax.axis_size("dp") // (2 * len(X_ORDER))
    chips = [z * len(X_ORDER) + x for z in reversed(range(rows)) for x in X_ORDER]
    groups = [[2 * chip + core for chip in chips] for core in range(2)]
    return lax.all_to_all(value, "dp", 0, 0, axis_index_groups=groups)


def merge_kernel(half_ref, grads, error, out, grad_buf, error_buf, sems):
    chips = out.shape[0]
    pieces = grad_buf.shape[0]
    width = grad_buf.shape[2]
    start = half_ref[0] * (chips * LANES)
    copies = []
    for i in range(pieces):
        at = pl.ds(pl.multiple_of(start + i * width, LANES), width)
        one = pltpu.make_async_copy(grads.at[:, at], grad_buf.at[i], sems.at[0, i])
        two = pltpu.make_async_copy(error.at[:, at], error_buf.at[i], sems.at[1, i])
        one.start()
        two.start()
        copies.append((one, two))
    for i in range(pieces):
        for copy in copies[i]:
            copy.wait()
        for j in range(width // LANES):
            at = slice(j * LANES, (j + 1) * LANES)
            out[i * (width // LANES) + j] = grad_buf[i, :, at].astype(jnp.float32) + error_buf[i, :, at]


def merged_half(half, grads, error):
    cols, depth = grads.shape
    chips = depth // (2 * LANES)
    pieces = 2
    width = depth // 2 // pieces
    return pl.pallas_call(
        merge_kernel,
        out_shape=jax.ShapeDtypeStruct((chips, cols, LANES), jnp.float32),
        in_specs=[SMEM, HBM, HBM],
        out_specs=VMEM,
        scratch_shapes=[
            pltpu.VMEM((pieces, cols, width), grads.dtype),
            pltpu.VMEM((pieces, cols, width), jnp.float32),
            pltpu.SemaphoreType.DMA((2, pieces)),
        ],
        compiler_params=pltpu.CompilerParams(vmem_limit_bytes=VMEM_LIMIT),
        cost_estimate=pl.CostEstimate(flops=cols * depth, bytes_accessed=5 * cols * depth, transcendentals=0),
        name="merge",
    )(half.reshape(1), *(pltpu.with_memory_space_constraint(x, pltpu.HBM) for x in (grads, error)))


def message_kernel(parts, total, out):
    chips, tiles = out.shape[:2]
    left = parts[0]
    for i in range(1, parts.shape[0]):
        left = left + parts[i]
    scaled = left / peak_of(left)
    small = lax.dot_general(scaled, total[...], (((1,), (1,)), ((), ())), precision=HIGHEST, preferred_element_type=jnp.float32)
    small = jnp.concatenate([small, jnp.zeros((small.shape[0], LANES - small.shape[1]), jnp.float32)], axis=1)
    lane = lax.broadcasted_iota(jnp.int32, (TILE, LANES), 1)
    packed = small[:TILE]
    for j in range(1, tiles - 1):
        piece = pltpu.roll(small, j * QUARTER, 1)[j * TILE : (j + 1) * TILE]
        packed = jnp.where(lane >= j * QUARTER, piece, packed)
    pieces = [left[j * TILE : (j + 1) * TILE] for j in range(tiles - 1)] + [packed]
    for i in range(chips):
        for j in range(tiles):
            out[i, j] = pieces[j]


def message_of(parts, total, chips):
    tiles = parts.shape[1] // TILE + 1
    return pl.pallas_call(
        message_kernel,
        out_shape=jax.ShapeDtypeStruct((chips, tiles, TILE, LANES), jnp.float32),
        in_specs=[VMEM, VMEM],
        out_specs=VMEM,
        compiler_params=pltpu.CompilerParams(vmem_limit_bytes=VMEM_LIMIT),
        name="message",
    )(parts, total)


def peak_of(left):
    peak = jnp.max(jnp.max(jnp.abs(left), axis=1, keepdims=True), axis=0, keepdims=True)
    return jnp.maximum(peak, 1e-30) * 128.0


def split3(value):
    first = value.astype(jnp.bfloat16)
    rest = value - first.astype(jnp.float32)
    second = rest.astype(jnp.bfloat16)
    third = (rest - second.astype(jnp.float32)).astype(jnp.bfloat16)
    return first, second, third


def left_of(message, i):
    tiles = message.shape[1] - 1
    return jnp.concatenate([message[i, j] for j in range(tiles)], axis=0)


def sums_of(message):
    chips, tiles = message.shape[0], message.shape[1] - 1
    rank = tiles * TILE
    square = jnp.zeros((3 * rank, 3 * rank), jnp.float32)
    peaks = []
    for i in range(0, chips, 2):
        pair = [left_of(message, i), left_of(message, i + 1)]
        peaks += [jnp.broadcast_to(peak_of(left), (1, LANES)) for left in pair]
        terms = jnp.concatenate(split3(jnp.concatenate(pair, axis=1)), axis=0)
        square += lax.dot_general(terms, terms, (((1,), (1,)), ((), ())), preferred_element_type=jnp.float32)
    at = [slice(i * rank, (i + 1) * rank) for i in range(3)]
    cross = square[at[0], at[2]] + square[at[2], at[0]] + square[at[1], at[1]]
    cross = cross + (square[at[0], at[1]] + square[at[1], at[0]])
    gram = square[at[0], at[0]] + cross
    gram = jnp.concatenate([gram, jnp.zeros((rank, LANES - rank), jnp.float32)], axis=1)
    peak = functools.reduce(jnp.maximum, peaks)
    inverse = 1.0 / peak
    small = functools.reduce(jnp.add, [message[i, tiles] * (peaks[i] * inverse) for i in range(chips)])
    small = jnp.concatenate([small] + [pltpu.roll(small, LANES - j * QUARTER, 1) for j in range(1, tiles)], axis=0)
    return gram, small, peak


def half_kernel(message, gram_ref, small_ref, peak_ref):
    gram_ref[...], small_ref[...], peak = sums_of(message)
    peak_ref[...] = jnp.broadcast_to(peak, peak_ref.shape)


def half_sums(message):
    rank = (message.shape[1] - 1) * TILE
    shape = jax.ShapeDtypeStruct((rank, LANES), jnp.float32)
    return pl.pallas_call(
        half_kernel,
        out_shape=(shape, shape, jax.ShapeDtypeStruct((8, LANES), jnp.float32)),
        in_specs=[VMEM],
        out_specs=(VMEM, VMEM, VMEM),
        compiler_params=pltpu.CompilerParams(vmem_limit_bytes=VMEM_LIMIT),
        cost_estimate=pl.CostEstimate(flops=message.size * rank, bytes_accessed=4 * message.size, transcendentals=0),
        name="half_sums",
    )(message)


def solve(own, got, replicas):
    shape = own[0].shape
    rank = shape[0]
    gram = own[0] + got[0]
    peak = jnp.maximum(own[2], got[2])
    small = own[1] * (own[2] / peak) + got[1] * (got[2] / peak)
    row = lax.broadcasted_iota(jnp.int32, shape, 0)
    column = [jnp.broadcast_to(gram[:, j : j + 1], shape) for j in range(rank)]
    trace = column[0][:1]
    for j in range(1, rank):
        trace = trace + column[j][j : j + 1]
    ridge = 1e-06 * trace / rank
    column = [jnp.where(row == j, column[j] + ridge, column[j]) for j in range(rank)]
    root = jnp.zeros(shape, jnp.float32)
    for k in range(rank):
        pivot = column[k][k : k + 1]
        inverse = lax.rsqrt(pivot)
        root = jnp.where(row == k, inverse, root)
        factor = jnp.where(row > k, column[k] * inverse * inverse, 0.0)
        for j in range(k + 1, rank):
            column[j] = column[j] - factor * column[j][k : k + 1]
        small = small - factor * small[k : k + 1]
    scale = peak * root
    new_q = small * (scale * (1.0 / replicas))
    coef = new_q * scale
    for k in range(rank - 1, 0, -1):
        upper = jnp.where(row < k, column[k] * root * root, 0.0)
        coef = coef - upper * coef[k : k + 1]
    return new_q, coef, 1.0 / peak


def finish_kernel(replicas, core_ref, own, got, gram, small, peak, mine, other, update, residual, new_q_ref,
                  update_buf, residual_buf, sems):
    chips, cols = mine.shape[:2]
    span = chips * LANES
    pieces = sems.shape[2]
    width = span // pieces
    starts = [pl.multiple_of(core_ref[0] * span, LANES), pl.multiple_of((1 - core_ref[0]) * span, LANES)]
    new_q, coef, inverse = solve((gram[...], small[...], peak[:1]), sums_of(got), replicas)
    new_q_ref[...] = new_q[:, :cols]
    first, second, third = split3(coef)
    lhs = jnp.concatenate([first, first, second, first, second, third], axis=0)
    lhs = jnp.transpose(lhs.astype(jnp.float32))[:cols].astype(jnp.bfloat16)
    stores = []
    for h, (source, merged) in enumerate(((own, mine), (got, other))):
        for i in range(0, chips, 2):
            left = jnp.concatenate([left_of(source, i) * inverse, left_of(source, i + 1) * inverse], axis=1)
            one, two, three = split3(left)
            rhs = jnp.concatenate([one, two, one, three, two, one], axis=0)
            approx = jnp.dot(lhs, rhs, preferred_element_type=jnp.float32)
            at = slice(i * LANES, (i + 2) * LANES)
            update_buf[h, :, at] = approx.astype(jnp.bfloat16)
            residual_buf[h, :, at] = jnp.concatenate([merged[i], merged[i + 1]], axis=1) - approx
            done = (i + 2) * LANES
            if done % width == 0:
                piece = done // width - 1
                here = pl.ds(piece * width, width)
                there = pl.ds(pl.multiple_of(starts[h] + piece * width, LANES), width)
                one = pltpu.make_async_copy(update_buf.at[h, :, here], update.at[:, there], sems.at[0, h, piece])
                two = pltpu.make_async_copy(residual_buf.at[h, :, here], residual.at[:, there], sems.at[1, h, piece])
                one.start()
                two.start()
                stores += [one, two]
    for copy in stores:
        copy.wait()


def finish(core, own, got, sums, mine, other, replicas):
    chips, cols = mine.shape[:2]
    rank = sums[0].shape[0]
    span = chips * LANES
    pieces = 2
    return pl.pallas_call(
        functools.partial(finish_kernel, replicas),
        out_shape=(
            jax.ShapeDtypeStruct((cols, 2 * span), jnp.bfloat16),
            jax.ShapeDtypeStruct((cols, 2 * span), jnp.float32),
            jax.ShapeDtypeStruct((rank, cols), jnp.float32),
        ),
        in_specs=[SMEM] + [VMEM] * 7,
        out_specs=(ANY, ANY, VMEM),
        scratch_shapes=[
            pltpu.VMEM((2, cols, span), jnp.bfloat16),
            pltpu.VMEM((2, cols, span), jnp.float32),
            pltpu.SemaphoreType.DMA((2, 2, pieces)),
        ],
        compiler_params=pltpu.CompilerParams(vmem_limit_bytes=VMEM_LIMIT),
        name="finish",
    )(core.reshape(1), own, got, *sums, mine, other)


def per_device(grads, error, q_init):
    replicas = lax.axis_size("dp")
    shards = lax.axis_size("tensor")
    chips = replicas // 2
    rank = q_init.shape[1]
    grads, error = grads[0], error[0]
    core = lax.axis_index("dp") % 2
    other = merged_half(1 - core, grads, error)
    swapped = swap_cores(other)
    mine = merged_half(core, grads, error)
    total = across_chips(mine + swapped).sum(0)
    part = jnp.dot(q_init.T, total, precision=HIGHEST)
    order = [i for i in TENSOR_ORDER if i < shards]
    parts = lax.all_to_all(jnp.broadcast_to(part, (shards, rank, LANES)), "tensor", 0, 0, axis_index_groups=[order])
    own = across_chips(message_of(parts, total, chips))
    got = swap_cores(own)
    update, residual, new_q = finish(core, own, got, half_sums(own), mine, other, replicas)
    return update, residual[None], new_q.T


def solution(mesh):
    in_specs = (P("dp", "tensor", None), P("dp", "tensor", None), P("tensor", None))
    out_specs = (P("tensor", None), P("dp", "tensor", None), P("tensor", None))
    return jax.shard_map(
        per_device, mesh=mesh, in_specs=in_specs, out_specs=out_specs, check_vma=False
    )
```
